32 devices in a mesh: groups: 2 (over y), feat: 4 (over z), layer: 2 (over x), row: 2 (over core).
Axes of the slice: x: 2, y: 2, z: 4, core: 2. Of those that a mesh axis runs over, the one named last changes fastest.
Arguments:
- resid_buf: bfloat16 [512, 2, 4608], P(('groups', 'feat', 'row')), parts along dimension 0, may hold values from -6 to 6
- shuffle: int32 [512], P('groups'), parts along dimension 0, may hold values from 0 to 255, each once
- mlp_out: bfloat16 [512, 2, 4608], P(('groups', 'feat', 'row')), parts along dimension 0, may hold values from -5 to 5
- enc_weight: bfloat16 [2, 8192, 4608], P('layer', 'feat', 'row'), may hold values from -0.09375 to 0.09375
- dec_weight: bfloat16 [2, 8192, 2, 4608], P('layer', 'feat', None, 'row'), may hold values from -0.0625 to 0.0625
- enc_bias: float32 [2, 8192], P('layer', 'feat'), may hold values from -0.5 to 0.5
- dec_bias: float32 [2, 4608], replicated, may hold values from -3 to 3
Outputs:
- rebuilt: bfloat16 [512, 2, 4608], P(('groups', 'feat', 'row')), parts along dimension 0
- enc_grad: bfloat16 [4, 8192, 4608], P(('groups', 'layer'), 'feat', 'row'), parts along dimension 0
- dec_grad: bfloat16 [4, 8192, 2, 4608], P(('groups', 'layer'), 'feat', None, 'row'), parts along dimension 0
- bias_grad: float32 [4, 8192], P(('groups', 'layer'), 'feat'), parts along dimension 0
The draws below stay inside these ranges and needn't reach their ends.
There are 2 independent parts, one for each index of `groups`. The reference program is written for one: setup_inputs(seed, part) draws one part's arguments, and reference() takes and returns one part's arrays. A program takes and returns all parts, laid end to end along the dimension named above; an argument that names none is the same for every part. Nothing has to cross between parts.
Inputs may be any that keep to these rules, and one draw needn't show every extreme that they name: `shuffle`: a permutation of the 256 buffer rows.
All inputs are finite; a program needn't handle non-finite values.
Results may differ from the reference program's by a relative error of at most 0.04.
Values may be sent and summed in bfloat16 or wider, within the bound.
No kernel may reach another device: no remote copies, remote signals or barrier semaphores. Data moves between devices by JAX's collectives and lax.ppermute only.
A program may use at most 128 MiB of HBM per device.

```python
import jax
import jax.numpy as jnp

D = 4608
F = 8192
LAYERS = 2
ROWS = 256
FSEC = 8192
N_LAYER = 2


def steps_of(rng, shape, pieces, smallest, largest):
    def one(position, shards_of):
        steps = jax.random.uniform(jax.random.fold_in(jax.random.fold_in(rng, 6), position), (shards_of,), jnp.float32, smallest / len(pieces), largest / len(pieces))
        return jnp.repeat(jnp.exp(steps), shape[position] // shards_of).reshape((-1,) + (1,) * (len(shape) - position - 1))

    gain = one(*pieces[0])
    for cut in pieces[1:]:
        gain = gain * one(*cut)
    return gain


def centred(rng, shape, scale, limit, pieces=(), held_as=jnp.bfloat16):
    array = jax.random.normal(rng, shape, jnp.float32) * scale
    if len(pieces) > 0:
        array = steps_of(rng, shape, pieces, -0.22, 0.18) * array
    return jnp.clip(array, min=-limit, max=limit).astype(held_as)


def setup_inputs(seed: int = 0, part: int = 0) -> dict:
    seeds = jax.random.split(jax.random.key(seed), 8)
    own_keys = jax.random.split(jax.random.fold_in(seeds[7], part), 8)
    resid_buf = centred(own_keys[0], (ROWS, LAYERS, D), 1.0, 6.0, ((0, 8),))
    shuffle = jax.random.permutation(own_keys[1], ROWS).astype(jnp.int32)
    mlp_out = centred(own_keys[2], (ROWS, LAYERS, D), 0.7, 5.0, ((0, 8),))
    enc_weight = centred(seeds[3], (N_LAYER, FSEC, D), D ** -0.5, 0.09375, ((0, 2), (1, 4), (2, 2)))
    dec_weight = centred(seeds[4], (N_LAYER, FSEC, 2, D), F ** -0.5, 0.0625, ((0, 2), (1, 4), (3, 2)))
    enc_bias = jnp.clip(jax.random.uniform(seeds[5], (N_LAYER, FSEC), jnp.float32, -0.5, 0.5) * steps_of(seeds[5], (N_LAYER, FSEC), ((0, 2), (1, 4)), -0.4, 0.0), -0.5, 0.5)
    dec_bias = centred(seeds[6], (LAYERS, D), 0.5, 3.0, (), jnp.float32)
    return {"resid_buf": resid_buf, "shuffle": shuffle, "mlp_out": mlp_out, "enc_weight": enc_weight, "dec_weight": dec_weight, "enc_bias": enc_bias, "dec_bias": dec_bias}


def reference(resid_buf, shuffle, mlp_out, enc_weight, dec_weight, enc_bias, dec_bias):
    encoders = enc_weight.reshape(LAYERS, F, D)
    decoders = dec_weight.reshape(LAYERS, F, 2, D)
    biases = enc_bias.reshape(LAYERS, F)
    inputs = jnp.take(resid_buf, shuffle.astype(jnp.int32), axis=0)
    loss_scale = float(ROWS) ** -0.5
    pre_list = []
    feature_list = []
    for source in range(LAYERS):
        pre_act = jnp.dot(inputs[:, source], encoders[source].T, preferred_element_type=jnp.float32) + biases[source]
        pre_list.append(pre_act)
        feature_list.append(jnp.maximum(pre_act, 0.0).astype(jnp.bfloat16))
    rebuilt_list = []
    for target in range(LAYERS):
        total = jnp.zeros((ROWS, D), jnp.float32) + dec_bias[target]
        for source in range(target + 1):
            total = total + jnp.dot(feature_list[source], decoders[source, :, target - source], preferred_element_type=jnp.float32)
        rebuilt_list.append(total)
    recon_sum = jnp.stack(rebuilt_list, axis=1)
    errors = (recon_sum - mlp_out.astype(jnp.float32)).astype(jnp.bfloat16)
    enc_list = []
    dec_list = []
    bias_list = []
    for source in range(LAYERS):
        own_err = errors[:, source]
        grad_feats = jnp.dot(own_err, decoders[source, :, 0].T, preferred_element_type=jnp.float32)
        own_dec = loss_scale * jnp.dot(feature_list[source].T, own_err, preferred_element_type=jnp.float32)
        if source + 1 < LAYERS:
            next_err = errors[:, source + 1]
            grad_feats = grad_feats + jnp.dot(next_err, decoders[source, :, 1].T, preferred_element_type=jnp.float32)
            next_dec = loss_scale * jnp.dot(feature_list[source].T, next_err, preferred_element_type=jnp.float32)
        else:
            next_dec = jnp.zeros((F, D), jnp.float32)
        grad_feats = grad_feats * loss_scale
        grad_pre = jnp.where(pre_list[source] > 0, grad_feats, 0.0).astype(jnp.bfloat16)
        enc_list.append(jnp.dot(grad_pre.T, inputs[:, source], preferred_element_type=jnp.float32).astype(jnp.bfloat16))
        dec_list.append(jnp.stack([own_dec, next_dec], axis=1).astype(jnp.bfloat16))
        bias_list.append(jnp.sum(grad_pre.astype(jnp.float32), axis=0))
    enc_grad = jnp.stack(enc_list, axis=0).reshape(N_LAYER, FSEC, D)
    dec_grad = jnp.stack(dec_list, axis=0).reshape(N_LAYER, FSEC, 2, D)
    bias_grad = jnp.stack(bias_list, axis=0).reshape(N_LAYER, FSEC)
    return (recon_sum.astype(jnp.bfloat16), enc_grad, dec_grad, bias_grad)
```

```python
import functools

import jax
import jax.numpy as jnp
from jax import lax
from jax.experimental import pallas as pl
from jax.experimental.pallas import tpu as pltpu
from jax.sharding import PartitionSpec as P

CHUNKS = 2


def shifted(block, axis, distance):
    count = lax.axis_size(axis)
    return lax.ppermute(block, axis, [(i, (i + distance) % count) for i in range(count)])


def dot_last(left, right):
    return lax.dot_general(
        left, right, (((1,), (1,)), ((), ())), preferred_element_type=jnp.float32
    )


def dot_first(left, right):
    return lax.dot_general(
        left, right, (((0,), (0,)), ((), ())), preferred_element_type=jnp.float32
    )


def shift_order(count):
    return sorted(range(1, count), key=lambda k: -min(k, count - k))


def dec_grad_kernel(scale, features_ref, own_ref, next_ref, out_ref):
    features = features_ref[...]
    own = dot_first(features, own_ref[...])
    out_ref[:, 0, :] = (scale * own).astype(out_ref.dtype)
    following = dot_first(features, next_ref[...])
    out_ref[:, 1, :] = (scale * following).astype(out_ref.dtype)


def dec_grad_call(features, own, following, scale):
    rows, count = features.shape
    width = own.shape[1]
    block = min(128, count)
    return pl.pallas_call(
        functools.partial(dec_grad_kernel, scale),
        grid=(count // block,),
        in_specs=[
            pl.BlockSpec((rows, block), lambda i: (0, i)),
            pl.BlockSpec((rows, width), lambda i: (0, 0)),
            pl.BlockSpec((rows, width), lambda i: (0, 0)),
        ],
        out_specs=pl.BlockSpec((block, 2, width), lambda i: (i, 0, 0)),
        out_shape=jax.ShapeDtypeStruct((count, 2, width), jnp.bfloat16),
        cost_estimate=pl.CostEstimate(
            flops=4 * rows * count * width,
            bytes_accessed=4 * count * width + 4 * rows * width + 2 * rows * count,
            transcendentals=0,
        ),
        compiler_params=pltpu.CompilerParams(vmem_limit_bytes=32 * 1024 * 1024),
    )(features, own, following)


def on_device(resid_buf, shuffle, mlp_out, enc_weight, dec_weight, enc_bias, dec_bias):
    f32, bf16 = jnp.float32, jnp.bfloat16
    feat_count = lax.axis_size("feat")
    layer_count = lax.axis_size("layer")
    layers = resid_buf.shape[1]
    sub_blocks = layer_count // layers
    feat_pos = lax.axis_index("feat")
    source = lax.axis_index("layer") // sub_blocks
    row_pos = lax.axis_index("row")
    first_core = row_pos == 0
    leading = source + 1 < layers
    rows_each, _, width = resid_buf.shape
    half = enc_weight.shape[2]
    piece = half // CHUNKS
    block_rows = rows_each * lax.axis_size("row")
    total_rows = block_rows * feat_count
    loss_scale = float(total_rows) ** (-0.5)
    order = shift_order(feat_count)

    def to_half(block):
        left, right = block[:, :half], block[:, half:]
        mine = jnp.where(first_core, left, right)
        got = shifted(jnp.where(first_core, right, left), "row", 1)
        return jnp.concatenate(
            [jnp.where(first_core, mine, got), jnp.where(first_core, got, mine)], axis=0
        )

    def from_half(block):
        upper, lower = block[:rows_each], block[rows_each:]
        mine = jnp.where(first_core, upper, lower)
        got = shifted(jnp.where(first_core, lower, upper), "row", 1)
        return jnp.concatenate(
            [jnp.where(first_core, mine, got), jnp.where(first_core, got, mine)], axis=1
        )

    def section_total(block):
        total = block
        for step in range(1, sub_blocks):
            pairs = [
                (i, (i // sub_blocks) * sub_blocks + (i + step) % sub_blocks)
                for i in range(layer_count)
            ]
            total = total + lax.ppermute(block, "layer", pairs)
        return total

    own_layer = jnp.where(leading, resid_buf[:, 0], resid_buf[:, layers - 1])
    own_block = to_half(own_layer)
    arrived = {0: own_block}
    for k in order:
        arrived[k] = shifted(own_block, "feat", k)
    buffered = jnp.concatenate([arrived[k] for k in range(feat_count)], axis=0)
    blocks = shuffle.reshape(feat_count, block_rows)
    relative = (feat_pos - jnp.arange(feat_count)) % feat_count
    wanted = jnp.take(blocks, relative, axis=0).reshape(total_rows)
    place = ((feat_pos - wanted // block_rows) % feat_count) * block_rows + wanted % block_rows
    picks = (place[:, None] == jnp.arange(total_rows)[None]).astype(bf16)
    inputs = jnp.dot(picks, buffered, preferred_element_type=f32).astype(bf16)

    mlp_half = [to_half(mlp_out[:, t]) for t in range(layers)]
    bias_half = lax.dynamic_slice_in_dim(dec_bias, row_pos * half, half, axis=1)
    own_dec = dec_weight[0][:, 0]
    next_dec = dec_weight[0][:, 1]

    partial_pre = dot_last(inputs, enc_weight[0])
    pre = partial_pre + shifted(partial_pre, "row", 1) + enc_bias
    features = jnp.maximum(pre, 0.0).astype(bf16)

    next_part = jnp.dot(features, next_dec, preferred_element_type=f32).astype(bf16)
    own_part = jnp.dot(features, own_dec, preferred_element_type=f32)
    sent_part = own_part.astype(bf16)
    forward = [(i, i + sub_blocks) for i in range(layer_count - sub_blocks)]
    backward = [(j, i) for i, j in forward]

    def rows_of(array, k):
        j = (feat_count - k) % feat_count
        return array[j * block_rows : (j + 1) * block_rows]

    columns = [slice(c * piece, (c + 1) * piece) for c in range(CHUNKS)]
    carried = [lax.ppermute(next_part[:, cols], "layer", forward) for cols in columns]
    own_sum = []
    for cols in columns:
        total = rows_of(own_part, 0)[:, cols]
        for k in order:
            total = total + shifted(rows_of(sent_part, k)[:, cols], "feat", k).astype(f32)
        own_sum.append(total)
    first_errors, last_errors, rebuilt = [], [], []
    for c, cols in enumerate(columns):
        recon_first = section_total(own_sum[c]) + bias_half[0, cols]
        error_first = (recon_first - mlp_half[0][:, cols].astype(f32)).astype(bf16)
        gathered = {0: error_first}
        total = own_sum[c] + rows_of(carried[c], 0).astype(f32)
        for k in order:
            got = shifted(jnp.where(leading, error_first, rows_of(carried[c], k)), "feat", k)
            gathered[k] = got
            total = total + got.astype(f32)
        recon_last = section_total(total) + bias_half[layers - 1, cols]
        error_last = (recon_last - mlp_half[layers - 1][:, cols].astype(f32)).astype(bf16)
        error_last = jnp.where(leading, lax.ppermute(error_last, "layer", backward), error_last)
        own_rebuilt = jnp.where(leading, recon_first, recon_last).astype(bf16)
        other = shifted(own_rebuilt, "layer", sub_blocks)
        rebuilt.append(
            (jnp.where(leading, own_rebuilt, other), jnp.where(leading, other, own_rebuilt))
        )
        first_errors.append(jnp.concatenate([gathered[k] for k in range(feat_count)], axis=0))
        last = {0: error_last}
        for k in order:
            last[k] = shifted(error_last, "feat", k)
        last_errors.append(jnp.concatenate([last[k] for k in range(feat_count)], axis=0))
    first_error = jnp.concatenate(first_errors, axis=1)
    last_error = jnp.concatenate(last_errors, axis=1)
    own_error = jnp.where(leading, first_error, last_error)
    next_error = jnp.where(leading, last_error, jnp.zeros_like(last_error))

    terms = dot_last(own_error, own_dec) + dot_last(next_error, next_dec)
    grad_feats = (terms + shifted(terms, "row", 1)) * loss_scale
    grad_pre = jnp.where(pre > 0, grad_feats, 0.0).astype(bf16)
    dec_grad = dec_grad_call(features, own_error, next_error, loss_scale)
    enc_grad = dot_first(grad_pre, inputs).astype(bf16)
    bias_grad = jnp.sum(grad_pre.astype(f32), axis=0)
    halves = [jnp.concatenate([piece_[t] for piece_ in rebuilt], axis=1) for t in range(layers)]
    output = jnp.stack([from_half(block) for block in halves], axis=1)
    return output, enc_grad[None], dec_grad[None], bias_grad[None]


def solution(mesh):
    return jax.shard_map(
        on_device,
        mesh=mesh,
        in_specs=(
            P(("groups", "feat", "row"), None, None),
            P("groups"),
            P(("groups", "feat", "row"), None, None),
            P("layer", "feat", "row"),
            P("layer", "feat", None, "row"),
            P("layer", "feat"),
            P(),
        ),
        out_specs=(
            P(("groups", "feat", "row"), None, None),
            P(("groups", "layer"), "feat", "row"),
            P(("groups", "layer"), "feat", None, "row"),
            P(("groups", "layer"), "feat"),
        ),
        check_vma=False,
    )
```

```python
import functools

import jax
import jax.numpy as jnp
from jax import lax
from jax.experimental import pallas as pl
from jax.experimental.pallas import tpu as pltpu
from jax.sharding import PartitionSpec as P

CHUNKS = 2


def shifted(block, axis, distance):
    count = lax.axis_size(axis)
    return lax.ppermute(block, axis, [(i, (i + distance) % count) for i in range(count)])


def dot_last(left, right):
    return lax.dot_general(
        left, right, (((1,), (1,)), ((), ())), preferred_element_type=jnp.float32
    )


def dot_first(left, right):
    return lax.dot_general(
        left, right, (((0,), (0,)), ((), ())), preferred_element_type=jnp.float32
    )


def shift_order(count):
    return sorted(range(1, count), key=lambda k: -min(k, count - k))


def vmem_params():
    return pltpu.CompilerParams(vmem_limit_bytes=24 * 1024 * 1024)


def encoder_kernel(inputs_ref, weight_ref, out_ref):
    count, half = weight_ref.shape
    rows = inputs_ref.shape[0]
    block = min(256, count)

    def product(weight_block, out_block):
        out_block[...] = dot_last(inputs_ref[...], weight_block[...])

    pltpu.emit_pipeline(
        product,
        grid=(count // block,),
        in_specs=[pl.BlockSpec((block, half), lambda i: (i, 0))],
        out_specs=[pl.BlockSpec((rows, block), lambda i: (0, i))],
    )(weight_ref, out_ref)


def encoder_call(inputs, weight):
    rows, count = inputs.shape[0], weight.shape[0]
    return pl.pallas_call(
        encoder_kernel,
        in_specs=[
            pl.BlockSpec(memory_space=pltpu.VMEM),
            pl.BlockSpec(memory_space=pltpu.HBM),
        ],
        out_specs=pl.BlockSpec(memory_space=pl.ANY),
        out_shape=jax.ShapeDtypeStruct((rows, count), jnp.float32),
        compiler_params=vmem_params(),
    )(inputs, weight)


def pair_kernel(first_ref, second_ref, out_ref):
    out_ref[:, 0, :] = first_ref[...]
    out_ref[:, 1, :] = second_ref[...]


def pair_call(first, second):
    rows, width = first.shape
    return pl.pallas_call(
        pair_kernel,
        out_shape=jax.ShapeDtypeStruct((rows, 2, width), first.dtype),
        compiler_params=vmem_params(),
    )(first, second)


def dec_grad_kernel(scale, features_ref, own_ref, next_ref, *rest):
    out_ref = rest[-1]
    features = features_ref[...]
    own = dot_first(features, own_ref[...])
    out_ref[:, 0, :] = (scale * own).astype(out_ref.dtype)
    following = dot_first(features, next_ref[...])
    out_ref[:, 1, :] = (scale * following).astype(out_ref.dtype)


def dec_grad_call(features, own, following, scale, chunk, chunks, before=None):
    rows, count = features.shape
    piece = own.shape[1]
    block = min(512, count)
    specs = [
        pl.BlockSpec((rows, block), lambda i: (0, i)),
        pl.BlockSpec((rows, piece), lambda i: (0, 0)),
        pl.BlockSpec((rows, piece), lambda i: (0, 0)),
    ]
    operands = [features, own, following]
    aliases = {}
    if before is not None:
        specs.append(pl.BlockSpec(memory_space=pl.ANY))
        operands.append(before)
        aliases = {3: 0}
    return pl.pallas_call(
        functools.partial(dec_grad_kernel, scale),
        grid=(count // block,),
        in_specs=specs,
        out_specs=pl.BlockSpec((block, 2, piece), lambda i: (i, 0, chunk)),
        out_shape=jax.ShapeDtypeStruct((count, 2, piece * chunks), jnp.bfloat16),
        input_output_aliases=aliases,
        cost_estimate=pl.CostEstimate(
            flops=4 * rows * count * piece,
            bytes_accessed=4 * count * piece + 4 * rows * piece + 2 * rows * count,
            transcendentals=0,
        ),
        compiler_params=vmem_params(),
    )(*operands)


def enc_grad_kernel(scale, mine_ref, other_ref, live_ref, inputs_ref, enc_ref, bias_ref):
    grad = (mine_ref[...].astype(jnp.float32) + other_ref[...].astype(jnp.float32)) * scale
    grad = jnp.where(live_ref[...].astype(jnp.float32) > 0, grad, 0.0).astype(jnp.bfloat16)
    bias_ref[...] = jnp.sum(grad.astype(jnp.float32), axis=0, keepdims=True)
    enc_ref[...] = dot_first(grad, inputs_ref[...]).astype(enc_ref.dtype)


def enc_grad_call(mine, other, live, inputs, scale):
    rows, count = mine.shape
    half = inputs.shape[1]
    block = min(512, count)
    columns = pl.BlockSpec((rows, block), lambda i: (0, i))
    return pl.pallas_call(
        functools.partial(enc_grad_kernel, scale),
        grid=(count // block,),
        in_specs=[columns, columns, columns, pl.BlockSpec((rows, half), lambda i: (0, 0))],
        out_specs=[
            pl.BlockSpec((block, half), lambda i: (i, 0)),
            pl.BlockSpec((1, block), lambda i: (0, i)),
        ],
        out_shape=[
            jax.ShapeDtypeStruct((count, half), jnp.bfloat16),
            jax.ShapeDtypeStruct((1, count), jnp.float32),
        ],
        cost_estimate=pl.CostEstimate(
            flops=2 * rows * count * half,
            bytes_accessed=2 * count * half + 6 * rows * count + 2 * rows * half,
            transcendentals=0,
        ),
        compiler_params=vmem_params(),
    )(mine, other, live, inputs)


def on_device(resid_buf, shuffle, mlp_out, enc_weight, dec_weight, enc_bias, dec_bias):
    f32, bf16 = jnp.float32, jnp.bfloat16
    feat_count = lax.axis_size("feat")
    layer_count = lax.axis_size("layer")
    layers = resid_buf.shape[1]
    sub_blocks = layer_count // layers
    feat_pos = lax.axis_index("feat")
    source = lax.axis_index("layer") // sub_blocks
    row_pos = lax.axis_index("row")
    first_core = row_pos == 0
    leading = source + 1 < layers
    rows_each, _, width = resid_buf.shape
    half = enc_weight.shape[2]
    piece = half // CHUNKS
    block_rows = rows_each * lax.axis_size("row")
    total_rows = block_rows * feat_count
    loss_scale = float(total_rows) ** (-0.5)
    order = shift_order(feat_count)

    def to_half(block):
        left, right = block[:, :half], block[:, half:]
        mine = jnp.where(first_core, left, right)
        got = shifted(jnp.where(first_core, right, left), "row", 1)
        return jnp.concatenate(
            [jnp.where(first_core, mine, got), jnp.where(first_core, got, mine)], axis=0
        )

    def from_half(block):
        upper, lower = block[:rows_each], block[rows_each:]
        mine = jnp.where(first_core, upper, lower)
        got = shifted(jnp.where(first_core, lower, upper), "row", 1)
        return jnp.concatenate(
            [jnp.where(first_core, mine, got), jnp.where(first_core, got, mine)], axis=1
        )

    def section_total(block):
        total = block
        for step in range(1, sub_blocks):
            pairs = [
                (i, (i // sub_blocks) * sub_blocks + (i + step) % sub_blocks)
                for i in range(layer_count)
            ]
            total = total + lax.ppermute(block, "layer", pairs)
        return total

    own_layer = jnp.where(leading, resid_buf[:, 0], resid_buf[:, layers - 1])
    own_block = to_half(own_layer)
    arrived = {0: own_block}
    for k in order:
        arrived[k] = shifted(own_block, "feat", k)
    own_mlp, sent_block = lax.optimization_barrier((mlp_out, own_block))
    mlp_half = [to_half(own_mlp[:, t]) for t in range(layers)]
    mlp_half, dec_weight = lax.optimization_barrier((mlp_half, dec_weight))
    slots = jnp.swapaxes(dec_weight[0], 0, 1)
    buffered = jnp.concatenate([arrived[k] for k in range(feat_count)], axis=0)
    buffered, slots, enc_weight = lax.optimization_barrier((buffered, slots, enc_weight))
    blocks = shuffle.reshape(feat_count, block_rows)
    relative = (feat_pos - jnp.arange(feat_count)) % feat_count
    wanted = jnp.take(blocks, relative, axis=0).reshape(total_rows)
    place = ((feat_pos - wanted // block_rows) % feat_count) * block_rows + wanted % block_rows
    picks = (place[:, None] == jnp.arange(total_rows)[None]).astype(bf16)
    inputs = jnp.dot(picks, buffered, preferred_element_type=f32).astype(bf16)

    bias_half = lax.dynamic_slice_in_dim(dec_bias, row_pos * half, half, axis=1)

    partial_pre = encoder_call(inputs, enc_weight[0])
    pre = partial_pre + shifted(partial_pre, "row", 1) + enc_bias
    features, live = lax.optimization_barrier(
        (jnp.maximum(pre, 0.0).astype(bf16), (pre > 0).astype(bf16))
    )

    next_part = jnp.dot(features, slots[1], preferred_element_type=f32).astype(bf16)
    own_part = jnp.dot(features, slots[0], preferred_element_type=f32)
    forward = [(i, i + sub_blocks) for i in range(layer_count - sub_blocks)]
    backward = [(j, i) for i, j in forward]
    low, high = slice(0, piece), slice(piece, half)

    def rows_of(array, k):
        j = (feat_count - k) % feat_count
        return array[j * block_rows : (j + 1) * block_rows]

    def move(pick):
        arriving = [None] * feat_count
        for k in order:
            arriving[k] = shifted(pick(k), "feat", k)
        return arriving

    def reduced(partial, arriving):
        total = rows_of(partial, 0).astype(f32)
        for k in order:
            total = total + arriving[k].astype(f32)
        return section_total(total)

    def joined(block, arriving):
        return jnp.concatenate([block] + arriving[1:], axis=0)

    def error_of(recon, t, cols):
        return (recon - mlp_half[t][:, cols].astype(f32)).astype(bf16)

    last = layers - 1
    carried = lax.ppermute(next_part[:, high], "layer", forward)
    low_part = jnp.where(leading, next_part[:, low].astype(f32), own_part[:, low])
    low_sent = low_part.astype(bf16)
    low_moved = move(lambda k: rows_of(low_sent, k))
    near = order[-1]
    low_moved[near], carried = lax.optimization_barrier((low_moved[near], carried))
    second_part = jnp.where(leading, own_part[:, low], own_part[:, high] + carried.astype(f32))
    second_sent = second_part.astype(bf16)
    second_moved = move(lambda k: rows_of(second_sent, k))
    low_sum = reduced(low_part, low_moved)
    low_total = low_sum + shifted(low_sum, "layer", sub_blocks)
    recon_last_low = low_total + bias_half[last, low]
    last_low = error_of(recon_last_low, last, low)
    second_sum = reduced(second_part, second_moved)
    recon_second = second_sum + jnp.where(leading, bias_half[0, low], bias_half[last, high])
    second_mlp = jnp.where(leading, mlp_half[0][:, low], mlp_half[last][:, high])
    second_error = (recon_second - second_mlp.astype(f32)).astype(bf16)
    high_sent = own_part[:, high].astype(bf16)
    third_moved = move(lambda k: jnp.where(leading, rows_of(high_sent, k), second_error))
    third_moved[near], fourth = lax.optimization_barrier((third_moved[near], last_low))
    fourth_moved = move(lambda k: fourth)
    last_high_all = lax.ppermute(joined(second_error, third_moved), "layer", backward)
    third_high_all = joined(second_error, third_moved)
    third_sum = reduced(own_part[:, high], third_moved)
    recon_third = third_sum + bias_half[0, high]
    third_error = error_of(recon_third, 0, high)
    recon_low, recon_high = recon_second.astype(bf16), recon_third.astype(bf16)
    other_half = shifted(recon_low, "layer", sub_blocks)
    lead_high = lax.ppermute(recon_high, "layer", forward)
    fourth_moved[near], other_half, fifth = lax.optimization_barrier(
        (fourth_moved[near], other_half, second_error)
    )
    fifth_moved = move(lambda k: fifth)
    fourth_all = joined(fourth, fourth_moved)
    first_rows = jnp.concatenate(
        [jnp.where(leading, recon_low, other_half), jnp.where(leading, recon_high, lead_high)], axis=1
    )
    last_rows = jnp.concatenate(
        [recon_last_low.astype(bf16), jnp.where(leading, other_half, recon_low)], axis=1
    )
    output = pair_call(from_half(first_rows), from_half(last_rows))
    empty = jnp.zeros((total_rows, piece), bf16)
    next_low = jnp.where(leading, fourth_all, empty)
    next_high = jnp.where(leading, last_high_all, empty)
    next_terms = dot_last(jnp.concatenate([next_low, next_high], axis=1), slots[1])
    fifth_moved[near], next_terms, output, live, sixth = lax.optimization_barrier(
        (fifth_moved[near], next_terms, output, live, third_error)
    )
    sixth_moved = move(lambda k: sixth)

    own_low = jnp.where(leading, joined(second_error, fifth_moved), fourth_all)
    sixth_moved[near], own_low = lax.optimization_barrier((sixth_moved[near], own_low))
    dec_low = dec_grad_call(features, own_low, next_low, loss_scale, 0, CHUNKS)
    early = next_terms
    sixth_moved, dec_low, early = lax.optimization_barrier((sixth_moved[1:], dec_low, early))
    own_high = jnp.where(leading, joined(third_error, [None] + sixth_moved), third_high_all)
    terms = (early + dot_last(jnp.concatenate([own_low, own_high], axis=1), slots[0])).astype(bf16)
    other_terms = shifted(terms, "row", 1)
    dec_grad = dec_grad_call(features, own_high, next_high, loss_scale, 1, CHUNKS, dec_low)
    enc_grad, bias_grad = enc_grad_call(terms, other_terms, live, inputs, loss_scale)
    return output, enc_grad[None], dec_grad[None], bias_grad


def solution(mesh):
    return jax.shard_map(
        on_device,
        mesh=mesh,
        in_specs=(
            P(("groups", "feat", "row"), None, None),
            P("groups"),
            P(("groups", "feat", "row"), None, None),
            P("layer", "feat", "row"),
            P("layer", "feat", None, "row"),
            P("layer", "feat"),
            P(),
        ),
        out_specs=(
            P(("groups", "feat", "row"), None, None),
            P(("groups", "layer"), "feat", "row"),
            P(("groups", "layer"), "feat", None, "row"),
            P(("groups", "layer"), "feat"),
        ),
        check_vma=False,
    )
```

```python
import functools

import jax
import jax.numpy as jnp
from jax import lax
from jax.experimental import pallas as pl
from jax.experimental.pallas import tpu as pltpu
from jax.sharding import PartitionSpec as P

CHUNKS = 2


def shifted(block, axis, distance):
    count = lax.axis_size(axis)
    return lax.ppermute(block, axis, [(i, (i + distance) % count) for i in range(count)])


def swapped(block, axis, distance):
    return lax.ppermute(block, axis, [(i, i ^ distance) for i in range(lax.axis_size(axis))])


def dot_last(left, right):
    return lax.dot_general(
        left, right, (((1,), (1,)), ((), ())), preferred_element_type=jnp.float32
    )


def dot_first(left, right):
    return lax.dot_general(
        left, right, (((0,), (0,)), ((), ())), preferred_element_type=jnp.float32
    )


def spread(block, axis, doubling):
    count = lax.axis_size(axis)
    held = {0: block}
    if doubling:
        distance = count // 2
        while distance:
            held.update({j ^ distance: swapped(held[j], axis, distance) for j in list(held)})
            distance //= 2
    else:
        for k in reversed(range(1, count)):
            held[k] = swapped(block, axis, k)
    return [held[j] for j in range(count)]


def vmem_params():
    return pltpu.CompilerParams(vmem_limit_bytes=24 * 1024 * 1024)


def encoder_kernel(inputs_ref, weight_ref, out_ref):
    count, half = weight_ref.shape
    rows = inputs_ref.shape[0]
    block = min(256, count)

    def product(weight_block, out_block):
        out_block[...] = dot_last(inputs_ref[...], weight_block[...])

    pltpu.emit_pipeline(
        product,
        grid=(count // block,),
        in_specs=[pl.BlockSpec((block, half), lambda i: (i, 0))],
        out_specs=[pl.BlockSpec((rows, block), lambda i: (0, i))],
    )(weight_ref, out_ref)


def encoder_call(inputs, weight):
    rows, count = inputs.shape[0], weight.shape[0]
    return pl.pallas_call(
        encoder_kernel,
        in_specs=[
            pl.BlockSpec(memory_space=pltpu.VMEM),
            pl.BlockSpec(memory_space=pltpu.HBM),
        ],
        out_specs=pl.BlockSpec(memory_space=pl.ANY),
        out_shape=jax.ShapeDtypeStruct((rows, count), jnp.float32),
        compiler_params=vmem_params(),
    )(inputs, weight)


def pair_kernel(first_ref, second_ref, out_ref):
    out_ref[:, 0, :] = first_ref[...]
    out_ref[:, 1, :] = second_ref[...]


def pair_call(first, second):
    rows, width = first.shape
    return pl.pallas_call(
        pair_kernel,
        out_shape=jax.ShapeDtypeStruct((rows, 2, width), first.dtype),
        compiler_params=vmem_params(),
    )(first, second)


def dec_grad_kernel(scale, features_ref, own_ref, next_ref, *rest):
    out_ref = rest[-1]
    features = features_ref[...]
    own = dot_first(features, own_ref[...])
    out_ref[:, 0, :] = (scale * own).astype(out_ref.dtype)
    following = dot_first(features, next_ref[...])
    out_ref[:, 1, :] = (scale * following).astype(out_ref.dtype)


def dec_grad_call(features, own, following, scale, chunk, chunks, before=None):
    rows, count = features.shape
    piece = own.shape[1]
    block = min(512, count)
    specs = [
        pl.BlockSpec((rows, block), lambda i: (0, i)),
        pl.BlockSpec((rows, piece), lambda i: (0, 0)),
        pl.BlockSpec((rows, piece), lambda i: (0, 0)),
    ]
    operands = [features, own, following]
    aliases = {}
    if before is not None:
        specs.append(pl.BlockSpec(memory_space=pl.ANY))
        operands.append(before)
        aliases = {3: 0}
    return pl.pallas_call(
        functools.partial(dec_grad_kernel, scale),
        grid=(count // block,),
        in_specs=specs,
        out_specs=pl.BlockSpec((block, 2, piece), lambda i: (i, 0, chunk)),
        out_shape=jax.ShapeDtypeStruct((count, 2, piece * chunks), jnp.bfloat16),
        input_output_aliases=aliases,
        cost_estimate=pl.CostEstimate(
            flops=4 * rows * count * piece,
            bytes_accessed=4 * count * piece + 4 * rows * piece + 2 * rows * count,
            transcendentals=0,
        ),
        compiler_params=vmem_params(),
    )(*operands)


def enc_grad_kernel(scale, mine_ref, other_ref, live_ref, inputs_ref, enc_ref, bias_ref):
    grad = (mine_ref[...].astype(jnp.float32) + other_ref[...].astype(jnp.float32)) * scale
    grad = jnp.where(live_ref[...].astype(jnp.float32) > 0, grad, 0.0).astype(jnp.bfloat16)
    bias_ref[...] = jnp.sum(grad.astype(jnp.float32), axis=0, keepdims=True)
    enc_ref[...] = dot_first(grad, inputs_ref[...]).astype(enc_ref.dtype)


def enc_grad_call(mine, other, live, inputs, scale):
    rows, count = mine.shape
    half = inputs.shape[1]
    block = min(512, count)
    columns = pl.BlockSpec((rows, block), lambda i: (0, i))
    return pl.pallas_call(
        functools.partial(enc_grad_kernel, scale),
        grid=(count // block,),
        in_specs=[columns, columns, columns, pl.BlockSpec((rows, half), lambda i: (0, 0))],
        out_specs=[
            pl.BlockSpec((block, half), lambda i: (i, 0)),
            pl.BlockSpec((1, block), lambda i: (0, i)),
        ],
        out_shape=[
            jax.ShapeDtypeStruct((count, half), jnp.bfloat16),
            jax.ShapeDtypeStruct((1, count), jnp.float32),
        ],
        cost_estimate=pl.CostEstimate(
            flops=2 * rows * count * half,
            bytes_accessed=2 * count * half + 6 * rows * count + 2 * rows * half,
            transcendentals=0,
        ),
        compiler_params=vmem_params(),
    )(mine, other, live, inputs)


def on_device(resid_buf, shuffle, mlp_out, enc_weight, dec_weight, enc_bias, dec_bias):
    f32, bf16 = jnp.float32, jnp.bfloat16
    feat_count = lax.axis_size("feat")
    layer_count = lax.axis_size("layer")
    layers = resid_buf.shape[1]
    sub_blocks = layer_count // layers
    feat_pos = lax.axis_index("feat")
    source = lax.axis_index("layer") // sub_blocks
    row_pos = lax.axis_index("row")
    first_core = row_pos == 0
    leading = source + 1 < layers
    rows_each, _, width = resid_buf.shape
    half = enc_weight.shape[2]
    piece = half // CHUNKS
    block_rows = rows_each * lax.axis_size("row")
    total_rows = block_rows * feat_count
    loss_scale = float(total_rows) ** (-0.5)
    others = range(1, feat_count)
    near = min(1, feat_count - 1)

    def to_half(block):
        left, right = block[:, :half], block[:, half:]
        mine = jnp.where(first_core, left, right)
        got = shifted(jnp.where(first_core, right, left), "row", 1)
        return jnp.concatenate(
            [jnp.where(first_core, mine, got), jnp.where(first_core, got, mine)], axis=0
        )

    def from_half(block):
        upper, lower = block[:rows_each], block[rows_each:]
        mine = jnp.where(first_core, upper, lower)
        got = shifted(jnp.where(first_core, lower, upper), "row", 1)
        return jnp.concatenate(
            [jnp.where(first_core, mine, got), jnp.where(first_core, got, mine)], axis=1
        )

    def section_total(block):
        total = block
        for step in range(1, sub_blocks):
            pairs = [
                (i, (i // sub_blocks) * sub_blocks + (i + step) % sub_blocks)
                for i in range(layer_count)
            ]
            total = total + lax.ppermute(block, "layer", pairs)
        return total

    own_layer = jnp.where(leading, resid_buf[:, 0], resid_buf[:, layers - 1])
    own_block = to_half(own_layer)
    arrived = spread(own_block, "feat", True)
    own_mlp, sent_block = lax.optimization_barrier((mlp_out, own_block))
    mlp_half = [to_half(own_mlp[:, t]) for t in range(layers)]
    mlp_half, dec_weight = lax.optimization_barrier((mlp_half, dec_weight))
    slots = jnp.swapaxes(dec_weight[0], 0, 1)
    buffered = jnp.concatenate(arrived, axis=0)
    buffered, slots, enc_weight = lax.optimization_barrier((buffered, slots, enc_weight))
    blocks = shuffle.reshape(feat_count, block_rows)
    relative = feat_pos ^ jnp.arange(feat_count)
    wanted = jnp.take(blocks, relative, axis=0).reshape(total_rows)
    place = (feat_pos ^ (wanted // block_rows)) * block_rows + wanted % block_rows
    picks = (place[:, None] == jnp.arange(total_rows)[None]).astype(bf16)
    inputs = jnp.dot(picks, buffered, preferred_element_type=f32).astype(bf16)

    bias_half = lax.dynamic_slice_in_dim(dec_bias, row_pos * half, half, axis=1)

    partial_pre = encoder_call(inputs, enc_weight[0])
    pre = partial_pre + shifted(partial_pre, "row", 1) + enc_bias
    features, live = lax.optimization_barrier(
        (jnp.maximum(pre, 0.0).astype(bf16), (pre > 0).astype(bf16))
    )

    next_part = jnp.dot(features, slots[1], preferred_element_type=f32).astype(bf16)
    own_part = jnp.dot(features, slots[0], preferred_element_type=f32)
    forward = [(i, i + sub_blocks) for i in range(layer_count - sub_blocks)]
    backward = [(j, i) for i, j in forward]
    low, high = slice(0, piece), slice(piece, half)

    def rows_of(array, k):
        return array[k * block_rows : (k + 1) * block_rows]

    def move(pick):
        arriving = [None] * feat_count
        for k in reversed(others):
            arriving[k] = swapped(pick(k), "feat", k)
        return arriving

    def reduced(partial, arriving):
        total = rows_of(partial, 0).astype(f32)
        for k in others:
            total = total + arriving[k].astype(f32)
        return section_total(total)

    def joined(block, arriving):
        return jnp.concatenate([block] + arriving[1:], axis=0)

    def error_of(recon, t, cols):
        return (recon - mlp_half[t][:, cols].astype(f32)).astype(bf16)

    last = layers - 1
    carried = lax.ppermute(next_part[:, high], "layer", forward)
    low_part = jnp.where(leading, next_part[:, low].astype(f32), own_part[:, low])
    low_sent = low_part.astype(bf16)
    low_moved = move(lambda k: rows_of(low_sent, k))
    low_moved[near], carried = lax.optimization_barrier((low_moved[near], carried))
    second_part = jnp.where(leading, own_part[:, low], own_part[:, high] + carried.astype(f32))
    second_sent = second_part.astype(bf16)
    second_moved = move(lambda k: rows_of(second_sent, k))
    low_sum = reduced(low_part, low_moved)
    low_total = low_sum + shifted(low_sum, "layer", sub_blocks)
    recon_last_low = low_total + bias_half[last, low]
    last_low = error_of(recon_last_low, last, low)
    second_sum = reduced(second_part, second_moved)
    recon_second = second_sum + jnp.where(leading, bias_half[0, low], bias_half[last, high])
    second_mlp = jnp.where(leading, mlp_half[0][:, low], mlp_half[last][:, high])
    second_error = (recon_second - second_mlp.astype(f32)).astype(bf16)
    high_sent = own_part[:, high].astype(bf16)
    third_moved = move(lambda k: jnp.where(leading, rows_of(high_sent, k), second_error))
    third_moved[near], fourth = lax.optimization_barrier((third_moved[near], last_low))
    fourth_moved = spread(fourth, "feat", True)
    last_high_all = lax.ppermute(joined(second_error, third_moved), "layer", backward)
    third_high_all = joined(second_error, third_moved)
    third_sum = reduced(own_part[:, high], third_moved)
    recon_third = third_sum + bias_half[0, high]
    third_error = error_of(recon_third, 0, high)
    recon_low, recon_high = recon_second.astype(bf16), recon_third.astype(bf16)
    other_half = shifted(recon_low, "layer", sub_blocks)
    lead_high = lax.ppermute(recon_high, "layer", forward)
    fourth_moved[near], other_half, fifth = lax.optimization_barrier(
        (fourth_moved[near], other_half, second_error)
    )
    fifth_moved = spread(fifth, "feat", True)
    fourth_all = joined(fourth, fourth_moved)
    first_rows = jnp.concatenate(
        [jnp.where(leading, recon_low, other_half), jnp.where(leading, recon_high, lead_high)], axis=1
    )
    last_rows = jnp.concatenate(
        [recon_last_low.astype(bf16), jnp.where(leading, other_half, recon_low)], axis=1
    )
    empty = jnp.zeros((total_rows, piece), bf16)
    next_low = jnp.where(leading, fourth_all, empty)
    next_high = jnp.where(leading, last_high_all, empty)
    next_terms = dot_last(jnp.concatenate([next_low, next_high], axis=1), slots[1])
    fifth_moved[near], next_terms, first_rows, last_rows, live, sixth = lax.optimization_barrier(
        (fifth_moved[near], next_terms, first_rows, last_rows, live, third_error)
    )
    sixth_moved = spread(sixth, "feat", False)

    own_low = jnp.where(leading, joined(second_error, fifth_moved), fourth_all)
    output = pair_call(from_half(first_rows), from_half(last_rows))
    output, own_low = lax.optimization_barrier((output, own_low))
    dec_low = dec_grad_call(features, own_low, next_low, loss_scale, 0, CHUNKS)
    early = next_terms
    sixth_moved, dec_low, early = lax.optimization_barrier((sixth_moved[1:], dec_low, early))
    own_high = jnp.where(leading, joined(third_error, [None] + sixth_moved), third_high_all)
    terms = (early + dot_last(jnp.concatenate([own_low, own_high], axis=1), slots[0])).astype(bf16)
    other_terms = shifted(terms, "row", 1)
    dec_grad = dec_grad_call(features, own_high, next_high, loss_scale, 1, CHUNKS, dec_low)
    enc_grad, bias_grad = enc_grad_call(terms, other_terms, live, inputs, loss_scale)
    return output, enc_grad[None], dec_grad[None], bias_grad


def solution(mesh):
    return jax.shard_map(
        on_device,
        mesh=mesh,
        in_specs=(
            P(("groups", "feat", "row"), None, None),
            P("groups"),
            P(("groups", "feat", "row"), None, None),
            P("layer", "feat", "row"),
            P("layer", "feat", None, "row"),
            P("layer", "feat"),
            P(),
        ),
        out_specs=(
            P(("groups", "feat", "row"), None, None),
            P(("groups", "layer"), "feat", "row"),
            P(("groups", "layer"), "feat", None, "row"),
            P(("groups", "layer"), "feat"),
        ),
        check_vma=False,
    )
```

```python
import functools

import jax
import jax.numpy as jnp
from jax import lax
from jax.experimental import pallas as pl
from jax.experimental.pallas import tpu as pltpu
from jax.sharding import PartitionSpec as P

CHUNKS = 2


def shifted(block, axis, distance):
    count = lax.axis_size(axis)
    return lax.ppermute(block, axis, [(i, (i + distance) % count) for i in range(count)])


def swapped(block, axis, distance):
    return lax.ppermute(block, axis, [(i, i ^ distance) for i in range(lax.axis_size(axis))])


def dot_last(left, right):
    return lax.dot_general(
        left, right, (((1,), (1,)), ((), ())), preferred_element_type=jnp.float32
    )


def dot_first(left, right):
    return lax.dot_general(
        left, right, (((0,), (0,)), ((), ())), preferred_element_type=jnp.float32
    )


def spread(block, axis, doubling):
    count = lax.axis_size(axis)
    held = {0: block}
    if doubling:
        distance = count // 2
        while distance:
            held.update({j ^ distance: swapped(held[j], axis, distance) for j in list(held)})
            distance //= 2
    else:
        for k in reversed(range(1, count)):
            held[k] = swapped(block, axis, k)
    return [held[j] for j in range(count)]


def vmem_params():
    return pltpu.CompilerParams(vmem_limit_bytes=24 * 1024 * 1024)


def encoder_kernel(part, inputs_ref, weight_ref, out_ref):
    rows, count = out_ref.shape
    half = weight_ref.shape[1]
    block = min(256, count)
    first = part * (count // block)

    def product(weight_block, out_block):
        out_block[...] = dot_last(inputs_ref[...], weight_block[...])

    pltpu.emit_pipeline(
        product,
        grid=(count // block,),
        in_specs=[pl.BlockSpec((block, half), lambda i: (first + i, 0))],
        out_specs=[pl.BlockSpec((rows, block), lambda i: (0, i))],
    )(weight_ref, out_ref)


def encoder_call(inputs, weight, part, parts):
    rows, count = inputs.shape[0], weight.shape[0] // parts
    return pl.pallas_call(
        functools.partial(encoder_kernel, part),
        in_specs=[
            pl.BlockSpec(memory_space=pltpu.VMEM),
            pl.BlockSpec(memory_space=pltpu.HBM),
        ],
        out_specs=pl.BlockSpec(memory_space=pl.ANY),
        out_shape=jax.ShapeDtypeStruct((rows, count), jnp.float32),
        compiler_params=vmem_params(),
    )(inputs, weight)


def pair_kernel(first_ref, second_ref, out_ref):
    out_ref[:, 0, :] = first_ref[...]
    out_ref[:, 1, :] = second_ref[...]


def pair_call(first, second):
    rows, width = first.shape
    return pl.pallas_call(
        pair_kernel,
        out_shape=jax.ShapeDtypeStruct((rows, 2, width), first.dtype),
        compiler_params=vmem_params(),
    )(first, second)


def dec_grad_kernel(scale, features_ref, own_ref, next_ref, *rest):
    out_ref = rest[-1]
    features = features_ref[...]
    own = dot_first(features, own_ref[...])
    out_ref[:, 0, :] = (scale * own).astype(out_ref.dtype)
    following = dot_first(features, next_ref[...])
    out_ref[:, 1, :] = (scale * following).astype(out_ref.dtype)


def dec_grad_call(features, own, following, scale, chunk, chunks, before=None):
    rows, count = features.shape
    piece = own.shape[1]
    block = min(512, count)
    specs = [
        pl.BlockSpec((rows, block), lambda i: (0, i)),
        pl.BlockSpec((rows, piece), lambda i: (0, 0)),
        pl.BlockSpec((rows, piece), lambda i: (0, 0)),
    ]
    operands = [features, own, following]
    aliases = {}
    if before is not None:
        specs.append(pl.BlockSpec(memory_space=pl.ANY))
        operands.append(before)
        aliases = {3: 0}
    return pl.pallas_call(
        functools.partial(dec_grad_kernel, scale),
        grid=(count // block,),
        in_specs=specs,
        out_specs=pl.BlockSpec((block, 2, piece), lambda i: (i, 0, chunk)),
        out_shape=jax.ShapeDtypeStruct((count, 2, piece * chunks), jnp.bfloat16),
        input_output_aliases=aliases,
        cost_estimate=pl.CostEstimate(
            flops=4 * rows * count * piece,
            bytes_accessed=4 * count * piece + 4 * rows * piece + 2 * rows * count,
            transcendentals=0,
        ),
        compiler_params=vmem_params(),
    )(*operands)


def enc_grad_kernel(scale, mine_ref, other_ref, live_ref, inputs_ref, enc_ref, bias_ref):
    grad = (mine_ref[...].astype(jnp.float32) + other_ref[...].astype(jnp.float32)) * scale
    grad = jnp.where(live_ref[...].astype(jnp.float32) > 0, grad, 0.0).astype(jnp.bfloat16)
    bias_ref[...] = jnp.sum(grad.astype(jnp.float32), axis=0, keepdims=True)
    enc_ref[...] = dot_first(grad, inputs_ref[...]).astype(enc_ref.dtype)


def enc_grad_call(mine, other, live, inputs, scale):
    rows, count = mine.shape
    half = inputs.shape[1]
    block = min(512, count)
    columns = pl.BlockSpec((rows, block), lambda i: (0, i))
    return pl.pallas_call(
        functools.partial(enc_grad_kernel, scale),
        grid=(count // block,),
        in_specs=[columns, columns, columns, pl.BlockSpec((rows, half), lambda i: (0, 0))],
        out_specs=[
            pl.BlockSpec((block, half), lambda i: (i, 0)),
            pl.BlockSpec((1, block), lambda i: (0, i)),
        ],
        out_shape=[
            jax.ShapeDtypeStruct((count, half), jnp.bfloat16),
            jax.ShapeDtypeStruct((1, count), jnp.float32),
        ],
        cost_estimate=pl.CostEstimate(
            flops=2 * rows * count * half,
            bytes_accessed=2 * count * half + 6 * rows * count + 2 * rows * half,
            transcendentals=0,
        ),
        compiler_params=vmem_params(),
    )(mine, other, live, inputs)


def on_device(resid_buf, shuffle, mlp_out, enc_weight, dec_weight, enc_bias, dec_bias):
    f32, bf16 = jnp.float32, jnp.bfloat16
    feat_count = lax.axis_size("feat")
    layer_count = lax.axis_size("layer")
    layers = resid_buf.shape[1]
    sub_blocks = layer_count // layers
    feat_pos = lax.axis_index("feat")
    source = lax.axis_index("layer") // sub_blocks
    row_pos = lax.axis_index("row")
    first_core = row_pos == 0
    leading = source + 1 < layers
    rows_each, _, width = resid_buf.shape
    half = enc_weight.shape[2]
    piece = half // CHUNKS
    block_rows = rows_each * lax.axis_size("row")
    total_rows = block_rows * feat_count
    loss_scale = float(total_rows) ** (-0.5)
    others = range(1, feat_count)
    near = min(1, feat_count - 1)

    def to_half(block):
        left, right = block[:, :half], block[:, half:]
        mine = jnp.where(first_core, left, right)
        got = shifted(jnp.where(first_core, right, left), "row", 1)
        return jnp.concatenate(
            [jnp.where(first_core, mine, got), jnp.where(first_core, got, mine)], axis=0
        )

    def from_half(block):
        upper, lower = block[:rows_each], block[rows_each:]
        mine = jnp.where(first_core, upper, lower)
        got = shifted(jnp.where(first_core, lower, upper), "row", 1)
        return jnp.concatenate(
            [jnp.where(first_core, mine, got), jnp.where(first_core, got, mine)], axis=1
        )

    def section_total(block):
        total = block
        for step in range(1, sub_blocks):
            pairs = [
                (i, (i // sub_blocks) * sub_blocks + (i + step) % sub_blocks)
                for i in range(layer_count)
            ]
            total = total + lax.ppermute(block, "layer", pairs)
        return total

    own_layer = jnp.where(leading, resid_buf[:, 0], resid_buf[:, layers - 1])
    own_block = to_half(own_layer)
    arrived = spread(own_block, "feat", True)
    own_mlp, sent_block = lax.optimization_barrier((mlp_out, own_block))
    mlp_half = [to_half(own_mlp[:, t]) for t in range(layers)]
    mlp_half, dec_weight = lax.optimization_barrier((mlp_half, dec_weight))
    slots = jnp.swapaxes(dec_weight[0], 0, 1)
    buffered = jnp.concatenate(arrived, axis=0)
    buffered, slots, enc_weight = lax.optimization_barrier((buffered, slots, enc_weight))
    blocks = shuffle.reshape(feat_count, block_rows)
    relative = feat_pos ^ jnp.arange(feat_count)
    wanted = jnp.take(blocks, relative, axis=0).reshape(total_rows)
    place = (feat_pos ^ (wanted // block_rows)) * block_rows + wanted % block_rows
    picks = (place[:, None] == jnp.arange(total_rows)[None]).astype(bf16)
    inputs = jnp.dot(picks, buffered, preferred_element_type=f32).astype(bf16)

    bias_half = lax.dynamic_slice_in_dim(dec_bias, row_pos * half, half, axis=1)

    feature_count = enc_weight.shape[1]
    parts = 2 if feature_count % 512 == 0 else 1
    sums = []
    for part in range(parts):
        partial_pre = encoder_call(inputs, enc_weight[0], part, parts)
        sums.append(partial_pre + shifted(partial_pre, "row", 1))
    pre = jnp.concatenate(sums, axis=1) + enc_bias
    features, live = lax.optimization_barrier(
        (jnp.maximum(pre, 0.0).astype(bf16), (pre > 0).astype(bf16))
    )

    next_part = jnp.dot(features, slots[1], preferred_element_type=f32).astype(bf16)
    own_part = jnp.dot(features, slots[0], preferred_element_type=f32)
    forward = [(i, i + sub_blocks) for i in range(layer_count - sub_blocks)]
    backward = [(j, i) for i, j in forward]
    low, high = slice(0, piece), slice(piece, half)

    def rows_of(array, k):
        return array[k * block_rows : (k + 1) * block_rows]

    def move(pick):
        arriving = [None] * feat_count
        for k in reversed(others):
            arriving[k] = swapped(pick(k), "feat", k)
        return arriving

    def reduced(partial, arriving):
        total = rows_of(partial, 0).astype(f32)
        for k in others:
            total = total + arriving[k].astype(f32)
        return section_total(total)

    def joined(block, arriving):
        return jnp.concatenate([block] + arriving[1:], axis=0)

    def error_of(recon, t, cols):
        return (recon - mlp_half[t][:, cols].astype(f32)).astype(bf16)

    last = layers - 1
    low_part = jnp.where(leading, next_part[:, low].astype(f32), own_part[:, low])
    low_sent = low_part.astype(bf16)
    low_sent, next_high_part = lax.optimization_barrier((low_sent, next_part[:, high]))
    low_moved = move(lambda k: rows_of(low_sent, k))
    carried = lax.ppermute(next_high_part, "layer", forward)
    low_moved[near], carried = lax.optimization_barrier((low_moved[near], carried))
    second_part = jnp.where(leading, own_part[:, low], own_part[:, high] + carried.astype(f32))
    second_sent = second_part.astype(bf16)
    second_moved = move(lambda k: rows_of(second_sent, k))
    low_sum = reduced(low_part, low_moved)
    low_total = low_sum + shifted(low_sum, "layer", sub_blocks)
    recon_last_low = low_total + bias_half[last, low]
    last_low = error_of(recon_last_low, last, low)
    second_sum = reduced(second_part, second_moved)
    recon_second = second_sum + jnp.where(leading, bias_half[0, low], bias_half[last, high])
    second_mlp = jnp.where(leading, mlp_half[0][:, low], mlp_half[last][:, high])
    second_error = (recon_second - second_mlp.astype(f32)).astype(bf16)
    high_sent = own_part[:, high].astype(bf16)
    third_moved = move(lambda k: jnp.where(leading, rows_of(high_sent, k), second_error))
    third_moved[near], fourth = lax.optimization_barrier((third_moved[near], last_low))
    fourth_moved = spread(fourth, "feat", True)
    last_high_all = lax.ppermute(joined(second_error, third_moved), "layer", backward)
    third_high_all = joined(second_error, third_moved)
    third_sum = reduced(own_part[:, high], third_moved)
    recon_third = third_sum + bias_half[0, high]
    third_error = error_of(recon_third, 0, high)
    recon_low, recon_high = recon_second.astype(bf16), recon_third.astype(bf16)
    other_half = shifted(recon_low, "layer", sub_blocks)
    lead_high = lax.ppermute(recon_high, "layer", forward)
    fourth_moved[near], other_half, fifth = lax.optimization_barrier(
        (fourth_moved[near], other_half, second_error)
    )
    fifth_moved = spread(fifth, "feat", True)
    fourth_all = joined(fourth, fourth_moved)
    first_rows = jnp.concatenate(
        [jnp.where(leading, recon_low, other_half), jnp.where(leading, recon_high, lead_high)], axis=1
    )
    last_rows = jnp.concatenate(
        [recon_last_low.astype(bf16), jnp.where(leading, other_half, recon_low)], axis=1
    )
    empty = jnp.zeros((total_rows, piece), bf16)
    next_low = jnp.where(leading, fourth_all, empty)
    next_high = jnp.where(leading, last_high_all, empty)
    next_terms = dot_last(jnp.concatenate([next_low, next_high], axis=1), slots[1])
    fifth_moved[near], next_terms, first_rows, last_rows, live, sixth = lax.optimization_barrier(
        (fifth_moved[near], next_terms, first_rows, last_rows, live, third_error)
    )
    sixth_moved = spread(sixth, "feat", False)

    own_low = jnp.where(leading, joined(second_error, fifth_moved), fourth_all)
    output = pair_call(from_half(first_rows), from_half(last_rows))
    output, own_low = lax.optimization_barrier((output, own_low))
    dec_low = dec_grad_call(features, own_low, next_low, loss_scale, 0, CHUNKS)
    early = next_terms
    sixth_moved, dec_low, early = lax.optimization_barrier((sixth_moved[1:], dec_low, early))
    own_high = jnp.where(leading, joined(third_error, [None] + sixth_moved), third_high_all)
    terms = (early + dot_last(jnp.concatenate([own_low, own_high], axis=1), slots[0])).astype(bf16)
    other_terms = shifted(terms, "row", 1)
    dec_grad = dec_grad_call(features, own_high, next_high, loss_scale, 1, CHUNKS, dec_low)
    enc_grad, bias_grad = enc_grad_call(terms, other_terms, live, inputs, loss_scale)
    return output, enc_grad[None], dec_grad[None], bias_grad


def solution(mesh):
    return jax.shard_map(
        on_device,
        mesh=mesh,
        in_specs=(
            P(("groups", "feat", "row"), None, None),
            P("groups"),
            P(("groups", "feat", "row"), None, None),
            P("layer", "feat", "row"),
            P("layer", "feat", None, "row"),
            P("layer", "feat"),
            P(),
        ),
        out_specs=(
            P(("groups", "feat", "row"), None, None),
            P(("groups", "layer"), "feat", "row"),
            P(("groups", "layer"), "feat", None, "row"),
            P(("groups", "layer"), "feat"),
        ),
        check_vma=False,
    )
```

```python
import functools
import math

import jax
import jax.numpy as jnp
from jax import lax
from jax.experimental import pallas as pl
from jax.experimental.pallas import tpu as pltpu
from jax.sharding import PartitionSpec as P

CHUNKS = 2


def shifted(block, axis, distance):
    count = lax.axis_size(axis)
    return lax.ppermute(block, axis, [(i, (i + distance) % count) for i in range(count)])


def swapped(block, axis, distance):
    return lax.ppermute(block, axis, [(i, i ^ distance) for i in range(lax.axis_size(axis))])


def dot_last(left, right):
    return lax.dot_general(
        left, right, (((1,), (1,)), ((), ())), preferred_element_type=jnp.float32
    )


def dot_first(left, right):
    return lax.dot_general(
        left, right, (((0,), (0,)), ((), ())), preferred_element_type=jnp.float32
    )


def spread(block, axis, doubling):
    count = lax.axis_size(axis)
    held = {0: block}
    if doubling:
        distance = count // 2
        while distance:
            held.update({j ^ distance: swapped(held[j], axis, distance) for j in list(held)})
            distance //= 2
    else:
        for k in reversed(range(1, count)):
            held[k] = swapped(block, axis, k)
    return [held[j] for j in range(count)]


def vmem_params():
    return pltpu.CompilerParams(vmem_limit_bytes=24 * 1024 * 1024)


def encoder_kernel(part, inputs_ref, weight_ref, out_ref):
    rows, count = out_ref.shape
    half = weight_ref.shape[1]
    block = min(256, count)
    first = part * (count // block)

    def product(weight_block, out_block):
        out_block[...] = dot_last(inputs_ref[...], weight_block[...])

    pltpu.emit_pipeline(
        product,
        grid=(count // block,),
        in_specs=[pl.BlockSpec((block, half), lambda i: (first + i, 0))],
        out_specs=[pl.BlockSpec((rows, block), lambda i: (0, i))],
    )(weight_ref, out_ref)


def encoder_call(inputs, weight, part, parts):
    rows, count = inputs.shape[0], weight.shape[0] // parts
    return pl.pallas_call(
        functools.partial(encoder_kernel, part),
        in_specs=[
            pl.BlockSpec(memory_space=pltpu.VMEM),
            pl.BlockSpec(memory_space=pltpu.HBM),
        ],
        out_specs=pl.BlockSpec(memory_space=pl.ANY),
        out_shape=jax.ShapeDtypeStruct((rows, count), jnp.float32),
        compiler_params=vmem_params(),
    )(inputs, weight)


def pair_kernel(first_ref, second_ref, out_ref):
    out_ref[:, 0, :] = first_ref[...]
    out_ref[:, 1, :] = second_ref[...]


def pair_call(first, second):
    rows, width = first.shape
    return pl.pallas_call(
        pair_kernel,
        out_shape=jax.ShapeDtypeStruct((rows, 2, width), first.dtype),
        compiler_params=vmem_params(),
    )(first, second)


def dec_grad_kernel(scale, features_ref, own_ref, next_ref, *rest):
    out_ref = rest[-1]
    features = features_ref[...]
    own, following = own_ref[...], next_ref[...]
    after = scale
    if math.log2(scale).is_integer():
        own, following, after = own * scale, following * scale, None

    def product(errors):
        found = dot_first(features, errors)
        return (found if after is None else after * found).astype(out_ref.dtype)

    out_ref[:, 0, :] = product(own)
    out_ref[:, 1, :] = product(following)


def dec_grad_call(features, own, following, scale, chunk, chunks, before=None):
    rows, count = features.shape
    piece = own.shape[1]
    block = min(512, count)
    specs = [
        pl.BlockSpec((rows, block), lambda i: (0, i)),
        pl.BlockSpec((rows, piece), lambda i: (0, 0)),
        pl.BlockSpec((rows, piece), lambda i: (0, 0)),
    ]
    operands = [features, own, following]
    aliases = {}
    if before is not None:
        specs.append(pl.BlockSpec(memory_space=pl.ANY))
        operands.append(before)
        aliases = {3: 0}
    return pl.pallas_call(
        functools.partial(dec_grad_kernel, scale),
        grid=(count // block,),
        in_specs=specs,
        out_specs=pl.BlockSpec((block, 2, piece), lambda i: (i, 0, chunk)),
        out_shape=jax.ShapeDtypeStruct((count, 2, piece * chunks), jnp.bfloat16),
        input_output_aliases=aliases,
        cost_estimate=pl.CostEstimate(
            flops=4 * rows * count * piece,
            bytes_accessed=4 * count * piece + 4 * rows * piece + 2 * rows * count,
            transcendentals=0,
        ),
        compiler_params=vmem_params(),
    )(*operands)


def enc_grad_kernel(scale, mine_ref, other_ref, live_ref, inputs_ref, enc_ref, bias_ref):
    grad = (mine_ref[...].astype(jnp.float32) + other_ref[...].astype(jnp.float32)) * scale
    grad = jnp.where(live_ref[...].astype(jnp.float32) > 0, grad, 0.0).astype(jnp.bfloat16)
    bias_ref[...] = jnp.sum(grad.astype(jnp.float32), axis=0, keepdims=True)
    enc_ref[...] = dot_first(grad, inputs_ref[...]).astype(enc_ref.dtype)


def enc_grad_call(mine, other, live, inputs, scale):
    rows, count = mine.shape
    half = inputs.shape[1]
    block = min(512, count)
    columns = pl.BlockSpec((rows, block), lambda i: (0, i))
    return pl.pallas_call(
        functools.partial(enc_grad_kernel, scale),
        grid=(count // block,),
        in_specs=[columns, columns, columns, pl.BlockSpec((rows, half), lambda i: (0, 0))],
        out_specs=[
            pl.BlockSpec((block, half), lambda i: (i, 0)),
            pl.BlockSpec((1, block), lambda i: (0, i)),
        ],
        out_shape=[
            jax.ShapeDtypeStruct((count, half), jnp.bfloat16),
            jax.ShapeDtypeStruct((1, count), jnp.float32),
        ],
        cost_estimate=pl.CostEstimate(
            flops=2 * rows * count * half,
            bytes_accessed=2 * count * half + 6 * rows * count + 2 * rows * half,
            transcendentals=0,
        ),
        compiler_params=vmem_params(),
    )(mine, other, live, inputs)


def on_device(resid_buf, shuffle, mlp_out, enc_weight, dec_weight, enc_bias, dec_bias):
    f32, bf16 = jnp.float32, jnp.bfloat16
    feat_count = lax.axis_size("feat")
    layer_count = lax.axis_size("layer")
    layers = resid_buf.shape[1]
    sub_blocks = layer_count // layers
    feat_pos = lax.axis_index("feat")
    source = lax.axis_index("layer") // sub_blocks
    row_pos = lax.axis_index("row")
    first_core = row_pos == 0
    leading = source + 1 < layers
    rows_each, _, width = resid_buf.shape
    half = enc_weight.shape[2]
    piece = half // CHUNKS
    block_rows = rows_each * lax.axis_size("row")
    total_rows = block_rows * feat_count
    loss_scale = float(total_rows) ** (-0.5)
    others = range(1, feat_count)
    near = min(1, feat_count - 1)

    def to_half(block):
        left, right = block[:, :half], block[:, half:]
        mine = jnp.where(first_core, left, right)
        got = shifted(jnp.where(first_core, right, left), "row", 1)
        return jnp.concatenate(
            [jnp.where(first_core, mine, got), jnp.where(first_core, got, mine)], axis=0
        )

    def from_half(block):
        upper, lower = block[:rows_each], block[rows_each:]
        mine = jnp.where(first_core, upper, lower)
        got = shifted(jnp.where(first_core, lower, upper), "row", 1)
        return jnp.concatenate(
            [jnp.where(first_core, mine, got), jnp.where(first_core, got, mine)], axis=1
        )

    def section_total(block):
        total = block
        for step in range(1, sub_blocks):
            pairs = [
                (i, (i // sub_blocks) * sub_blocks + (i + step) % sub_blocks)
                for i in range(layer_count)
            ]
            total = total + lax.ppermute(block, "layer", pairs)
        return total

    own_layer = jnp.where(leading, resid_buf[:, 0], resid_buf[:, layers - 1])
    own_block = to_half(own_layer)
    arrived = spread(own_block, "feat", True)
    own_mlp, sent_block = lax.optimization_barrier((mlp_out, own_block))
    mlp_half = [to_half(own_mlp[:, t]) for t in range(layers)]
    mlp_half, dec_weight = lax.optimization_barrier((mlp_half, dec_weight))
    slots = jnp.swapaxes(dec_weight[0], 0, 1)
    buffered = jnp.concatenate(arrived, axis=0)
    buffered, slots, enc_weight = lax.optimization_barrier((buffered, slots, enc_weight))
    blocks = shuffle.reshape(feat_count, block_rows)
    relative = feat_pos ^ jnp.arange(feat_count)
    wanted = jnp.take(blocks, relative, axis=0).reshape(total_rows)
    place = (feat_pos ^ (wanted // block_rows)) * block_rows + wanted % block_rows
    picks = (place[:, None] == jnp.arange(total_rows)[None]).astype(bf16)
    inputs = jnp.dot(picks, buffered, preferred_element_type=f32).astype(bf16)

    bias_half = lax.dynamic_slice_in_dim(dec_bias, row_pos * half, half, axis=1)

    feature_count = enc_weight.shape[1]
    parts = 2 if feature_count % 512 == 0 else 1
    sums = []
    for part in range(parts):
        partial_pre = encoder_call(inputs, enc_weight[0], part, parts)
        sums.append(partial_pre + shifted(partial_pre, "row", 1))
    pre = jnp.concatenate(sums, axis=1) + enc_bias
    features, live = lax.optimization_barrier(
        (jnp.maximum(pre, 0.0).astype(bf16), (pre > 0).astype(bf16))
    )

    next_part = jnp.dot(features, slots[1], preferred_element_type=f32).astype(bf16)
    own_part = jnp.dot(features, slots[0], preferred_element_type=f32)
    forward = [(i, i + sub_blocks) for i in range(layer_count - sub_blocks)]
    backward = [(j, i) for i, j in forward]
    low, high = slice(0, piece), slice(piece, half)

    def rows_of(array, k):
        return array[k * block_rows : (k + 1) * block_rows]

    def move(pick):
        arriving = [None] * feat_count
        for k in reversed(others):
            arriving[k] = swapped(pick(k), "feat", k)
        return arriving

    def reduced(partial, arriving):
        total = rows_of(partial, 0).astype(f32)
        for k in others:
            total = total + arriving[k].astype(f32)
        return section_total(total)

    def joined(block, arriving):
        return jnp.concatenate([block] + arriving[1:], axis=0)

    def error_of(recon, t, cols):
        return (recon - mlp_half[t][:, cols].astype(f32)).astype(bf16)

    last = layers - 1
    low_part = jnp.where(leading, next_part[:, low].astype(f32), own_part[:, low])
    low_sent = low_part.astype(bf16)
    low_sent, next_high_part = lax.optimization_barrier((low_sent, next_part[:, high]))
    low_moved = move(lambda k: rows_of(low_sent, k))
    carried = lax.ppermute(next_high_part, "layer", forward)
    low_moved[near], carried = lax.optimization_barrier((low_moved[near], carried))
    second_part = jnp.where(leading, own_part[:, low], own_part[:, high] + carried.astype(f32))
    second_sent = second_part.astype(bf16)
    second_moved = move(lambda k: rows_of(second_sent, k))
    low_sum = reduced(low_part, low_moved)
    low_total = low_sum + shifted(low_sum, "layer", sub_blocks)
    recon_last_low = low_total + bias_half[last, low]
    last_low = error_of(recon_last_low, last, low)
    second_sum = reduced(second_part, second_moved)
    recon_second = second_sum + jnp.where(leading, bias_half[0, low], bias_half[last, high])
    second_mlp = jnp.where(leading, mlp_half[0][:, low], mlp_half[last][:, high])
    second_error = (recon_second - second_mlp.astype(f32)).astype(bf16)
    high_sent = own_part[:, high].astype(bf16)
    third_moved = move(lambda k: jnp.where(leading, rows_of(high_sent, k), second_error))
    third_moved[near], fourth = lax.optimization_barrier((third_moved[near], last_low))
    fourth_moved = spread(fourth, "feat", True)
    last_high_all = lax.ppermute(joined(second_error, third_moved), "layer", backward)
    third_high_all = joined(second_error, third_moved)
    third_sum = reduced(own_part[:, high], third_moved)
    recon_third = third_sum + bias_half[0, high]
    third_error = error_of(recon_third, 0, high)
    recon_low, recon_high = recon_second.astype(bf16), recon_third.astype(bf16)
    other_half = shifted(recon_low, "layer", sub_blocks)
    lead_high = lax.ppermute(recon_high, "layer", forward)
    fourth_moved[near], other_half, fifth = lax.optimization_barrier(
        (fourth_moved[near], other_half, second_error)
    )
    fifth_moved = spread(fifth, "feat", True)
    fourth_all = joined(fourth, fourth_moved)
    first_rows = jnp.concatenate(
        [jnp.where(leading, recon_low, other_half), jnp.where(leading, recon_high, lead_high)], axis=1
    )
    last_rows = jnp.concatenate(
        [recon_last_low.astype(bf16), jnp.where(leading, other_half, recon_low)], axis=1
    )
    empty = jnp.zeros((total_rows, piece), bf16)
    next_low = jnp.where(leading, fourth_all, empty)
    next_high = jnp.where(leading, last_high_all, empty)
    next_terms = dot_last(jnp.concatenate([next_low, next_high], axis=1), slots[1])
    fifth_moved[near], next_terms, first_rows, last_rows, live, sixth = lax.optimization_barrier(
        (fifth_moved[near], next_terms, first_rows, last_rows, live, third_error)
    )
    sixth_moved = spread(sixth, "feat", False)

    own_low = jnp.where(leading, joined(second_error, fifth_moved), fourth_all)
    output = pair_call(from_half(first_rows), from_half(last_rows))
    output, own_low = lax.optimization_barrier((output, own_low))
    dec_low = dec_grad_call(features, own_low, next_low, loss_scale, 0, CHUNKS)
    early = next_terms
    sixth_moved, dec_low, early = lax.optimization_barrier((sixth_moved[1:], dec_low, early))
    own_high = jnp.where(leading, joined(third_error, [None] + sixth_moved), third_high_all)
    terms = (early + dot_last(jnp.concatenate([own_low, own_high], axis=1), slots[0])).astype(bf16)
    other_terms = shifted(terms, "row", 1)
    dec_grad = dec_grad_call(features, own_high, next_high, loss_scale, 1, CHUNKS, dec_low)
    enc_grad, bias_grad = enc_grad_call(terms, other_terms, live, inputs, loss_scale)
    return output, enc_grad[None], dec_grad[None], bias_grad


def solution(mesh):
    return jax.shard_map(
        on_device,
        mesh=mesh,
        in_specs=(
            P(("groups", "feat", "row"), None, None),
            P("groups"),
            P(("groups", "feat", "row"), None, None),
            P("layer", "feat", "row"),
            P("layer", "feat", None, "row"),
            P("layer", "feat"),
            P(),
        ),
        out_specs=(
            P(("groups", "feat", "row"), None, None),
            P(("groups", "layer"), "feat", "row"),
            P(("groups", "layer"), "feat", None, "row"),
            P(("groups", "layer"), "feat"),
        ),
        check_vma=False,
    )
```
